256 devices in a mesh: req: 2 (over core), seq: 128 (over y, z, x).
Axes of the slice: x: 4, y: 4, z: 8, core: 2. Of those that a mesh axis runs over, the one named last changes fastest.
Arguments:
- queries: bfloat16 [4, 8192], P('req'), parts along dimension 0, may hold values from -120 to 120
- new_tokens: bfloat16 [4, 2048], P('req'), parts along dimension 0, may hold values from -10.75 to 10.75
- cache_rows: bfloat16 [262144, 2048], P(('req', 'seq')), parts along dimension 0, may hold values from -4 to 4
- cache_length: int32 [2], P('req'), parts along dimension 0, may hold values from 65537 to 131072
- span_rows: bfloat16 [512, 512, 2048], P(('req', 'seq')), parts along dimension 0, may hold values from -6 to 6
- slot_blocks: int32 [512], P('req'), parts along dimension 0, may hold values from -1 to 31, as said below
- decode_owner: int32 [64], P('req'), parts along dimension 0, may hold values from 0 to 127, as said below
Outputs:
- attention: bfloat16 [4, 8192], P('req'), parts along dimension 0
- relaid_blocks: bfloat16 [256, 512, 2048], P(('req', 'seq')), parts along dimension 0
The draws below stay inside these ranges and needn't reach their ends.
There are 2 independent parts, one for each index of `req`. The reference program is written for one: setup_inputs(seed, part) draws one part's arguments, and reference() takes and returns one part's arrays. A program takes and returns all parts, laid end to end along the dimension named above; each array names one. Nothing has to cross between parts.
Inputs may be any that keep to these rules, and one draw needn't show every extreme that they name: `slot_blocks`: each block number 0 .. 31 stands in exactly one slot and -1 in all others; device i holds slots 2 * i .. 2 * i + 1, and some device has all its slots filled. `decode_owner`: the owners of different blocks are different devices.
All inputs are finite; a program needn't handle non-finite values.
Results may differ from the reference program's by a relative error of at most 0.0055.
Values may be sent and summed in bfloat16 or wider, within the bound.
No kernel may reach another device: no remote copies, remote signals or barrier semaphores. Data moves between devices by JAX's collectives and lax.ppermute only.
A program may use at most 128 MiB of HBM per device.

```python
import jax
import jax.numpy as jnp
from jax import lax

HEADS = 64
KV_HEADS = 8
HEAD_DIM = 128
CACHE_DEV = 1024
BLOCK = 512
SLOTS = 2
STEPS = 2
GROUP = 8
FEAT = 2048
SPAN_BLOCKS = 32
N_SEQ = 128


def anchors(key):
    head_key = jax.random.fold_in(key, 2)
    member_key = jax.random.fold_in(key, 3)
    extra_key = jax.random.fold_in(key, 4)
    groups = jax.random.permutation(head_key, KV_HEADS)[:2].astype(jnp.int32)
    members = jax.random.randint(member_key, (2,), 0, GROUP).astype(jnp.int32)
    marked = jnp.clip(jax.random.normal(extra_key, (HEAD_DIM,), jnp.float32), -2.0, 2.0)
    return (groups, members, marked)


def draw_queries(key, part):
    groups, members, marked = anchors(key)
    key = jax.random.fold_in(key, 1)
    values = 3.0 * jnp.clip(jax.random.normal(key, (STEPS, HEADS * HEAD_DIM), jnp.float32), -6.0, 6.0)
    other_member = (members[0] + 1) % GROUP
    column = ((groups[0] * GROUP + other_member) * HEAD_DIM).astype(jnp.int32)
    values = lax.dynamic_update_slice(values, (4.0 * marked)[None, :], (jnp.asarray(0, jnp.int32), column))
    values = jnp.clip(values, -120.0, 120.0)
    return values.astype(jnp.bfloat16)


def draw_cache_rows(key, part):
    groups, members, marked = anchors(key)
    key = jax.random.fold_in(key, 2)
    values = jnp.clip(jax.random.normal(key, (N_SEQ * CACHE_DEV, FEAT), jnp.float32), -4.0, 4.0)
    row = jnp.asarray(N_SEQ // 2 * CACHE_DEV, jnp.int32)
    column = (groups[0] * HEAD_DIM).astype(jnp.int32)
    values = lax.dynamic_update_slice(values, (1.9 * marked)[None, :], (row, column))
    return values.astype(jnp.bfloat16)


def draw_slot_blocks(key, part):
    key = jax.random.fold_in(key, 3)
    device_key, block_key, side_key = jax.random.split(key, 3)
    order = jax.random.permutation(device_key, N_SEQ).astype(jnp.int32)
    full_devices = order[:SPAN_BLOCKS // 4]
    half_devices = order[SPAN_BLOCKS // 4:SPAN_BLOCKS // 4 + SPAN_BLOCKS // 2]
    sides = jax.random.randint(side_key, (SPAN_BLOCKS // 2,), 0, SLOTS).astype(jnp.int32)
    targets = jnp.concatenate([full_devices * SLOTS, full_devices * SLOTS + 1, half_devices * SLOTS + sides])
    numbers = jax.random.permutation(block_key, SPAN_BLOCKS).astype(jnp.int32)
    return jnp.full((N_SEQ * SLOTS,), -1, jnp.int32).at[targets].set(numbers)


def draw_decode_owner(key, part):
    key = jax.random.fold_in(key, 4)
    middle_key, order_key = jax.random.split(key, 2)
    middle = jax.random.permutation(middle_key, N_SEQ - 2)[:SPAN_BLOCKS - 2].astype(jnp.int32) + 1
    owners = jnp.concatenate([jnp.array([0, N_SEQ - 1], jnp.int32), middle])
    return owners[jax.random.permutation(order_key, SPAN_BLOCKS)]


def steps_of(own_key, shape, pieces, low, high):
    factor_of = 1.0
    for position, blocks in pieces:
        steps = jax.random.uniform(jax.random.fold_in(jax.random.fold_in(own_key, 6), position), (blocks,), jnp.float32, low / len(pieces), high / len(pieces))
        factor_of = factor_of * jnp.repeat(jnp.exp(steps), shape[position] // blocks).reshape((-1,) + (1,) * (len(shape) - 1 - position))
    return factor_of


def centred(own_key, extent, spread, bound, pieces=(), kind=jnp.bfloat16):
    drawn = jax.random.normal(own_key, extent, jnp.float32) * spread
    if len(pieces) > 0:
        drawn = steps_of(own_key, extent, pieces, -0.22, 0.18) * drawn
    return jnp.clip(drawn, min=-bound, max=bound).astype(kind)


def setup_inputs(seed: int = 0, part: int = 0) -> dict:
    key_of = jax.random.split(jax.random.key(seed), 8)
    own_keys = jax.random.split(jax.random.fold_in(key_of[7], part), 8)
    queries = draw_queries(jax.random.fold_in(jax.random.fold_in(key_of[7], part), 71), part)
    new_tokens = centred(own_keys[1], (STEPS, FEAT), 1.8, 10.75)
    cache_rows = draw_cache_rows(jax.random.fold_in(jax.random.fold_in(key_of[7], part), 71), part)
    cache_length = jax.random.randint(own_keys[3], (1,), N_SEQ * CACHE_DEV // 2 + 1, N_SEQ * CACHE_DEV + 1).astype(jnp.int32)
    span_rows = centred(own_keys[4], (N_SEQ * SLOTS, BLOCK, FEAT), 1.0, 6.0, ((0, 128),))
    slot_blocks = draw_slot_blocks(jax.random.fold_in(jax.random.fold_in(key_of[7], part), 71), part)
    decode_owner = draw_decode_owner(jax.random.fold_in(jax.random.fold_in(key_of[7], part), 71), part)
    return {"queries": queries, "new_tokens": new_tokens, "cache_rows": cache_rows, "cache_length": cache_length, "span_rows": span_rows, "slot_blocks": slot_blocks, "decode_owner": decode_owner}


NEGATIVE = -1e30


def reference(queries, new_tokens, cache_rows, cache_length, span_rows, slot_blocks, decode_owner):
    block_count = decode_owner.shape[0]
    numbers = jnp.arange(block_count, dtype=jnp.int32)
    matches = slot_blocks[None, :] == numbers[:, None]
    holder = jnp.argmax(matches, axis=1).astype(jnp.int32)
    blocks = span_rows[holder]
    relaid_blocks = jnp.zeros((N_SEQ, BLOCK, FEAT), span_rows.dtype).at[decode_owner].set(blocks)
    all_rows = jnp.concatenate([cache_rows, blocks.reshape(-1, FEAT), new_tokens], axis=0)
    cached = cache_rows.shape[0]
    earlier_rows = cached + block_count * BLOCK
    row_index = jnp.arange(all_rows.shape[0], dtype=jnp.int32)[None, :]
    step_index = jnp.arange(STEPS, dtype=jnp.int32)[:, None]
    usable = (row_index < cache_length[0]) | ((row_index >= cached) & (row_index < earlier_rows)) | ((row_index >= earlier_rows) & (row_index - earlier_rows <= step_index))
    grouped = queries.reshape(STEPS, KV_HEADS, GROUP, HEAD_DIM).transpose(1, 0, 2, 3)

    def one_group(group_index):
        key_part = lax.dynamic_slice_in_dim(all_rows, group_index * HEAD_DIM, HEAD_DIM, 1).astype(jnp.float32)
        value_part = lax.dynamic_slice_in_dim(all_rows, (KV_HEADS + group_index) * HEAD_DIM, HEAD_DIM, 1).astype(jnp.float32)
        local_queries = lax.dynamic_index_in_dim(grouped, group_index, 0, keepdims=False).astype(jnp.float32)
        scores = jnp.einsum("shd,td->sht", local_queries, key_part) * (HEAD_DIM ** -0.5)
        scores = jnp.where(usable[:, None, :], scores, NEGATIVE)
        highest = jnp.max(scores, axis=2, keepdims=True)
        weights = jnp.where(usable[:, None, :], jnp.exp(scores - highest), 0.0)
        totals = jnp.sum(weights, axis=2)
        rounded = lax.optimization_barrier(weights.astype(jnp.bfloat16)).astype(jnp.float32)
        return jnp.einsum("sht,td->shd", rounded, value_part) / totals[..., None]

    outputs = lax.map(one_group, jnp.arange(KV_HEADS, dtype=jnp.int32))
    attention = outputs.transpose(1, 0, 2, 3).reshape(STEPS, HEADS * HEAD_DIM).astype(jnp.bfloat16)
    return attention, relaid_blocks
```

```python
import functools

import jax
import jax.numpy as jnp
from jax import lax
from jax.experimental import pallas as pl
from jax.experimental.pallas import tpu as pltpu
from jax.sharding import PartitionSpec as P

HEAD_DIM = 128
KV_HEADS = 8
TILE_ROWS = 8
NEGATIVE = -(2.0**99)


def halves(value):
    high = value.astype(jnp.bfloat16).astype(jnp.float32)
    low = (value - high).astype(jnp.bfloat16).astype(jnp.float32)
    return high, low


def attention_kernel(
    cache_tiles, span_tiles, live_ref, queries_ref, cache_ref, span_ref, new_ref, out_ref, blocks, total, stats
):
    step = pl.program_id(0)
    lanes = queries_ref.shape[0]
    per_head = lanes // KV_HEADS

    @pl.when(step == 0)
    def _():
        owner = lax.broadcasted_iota(jnp.int32, (lanes, HEAD_DIM), 0) // per_head
        queries = queries_ref[...].astype(jnp.float32)
        for head in range(KV_HEADS):
            blocks[:, head * HEAD_DIM : (head + 1) * HEAD_DIM] = jnp.where(owner == head, queries, 0.0).astype(
                jnp.bfloat16
            )
        total[...] = jnp.zeros_like(total)
        stats[0:1, :] = jnp.full((1, lanes), NEGATIVE, jnp.float32)
        stats[1:2, :] = jnp.zeros((1, lanes), jnp.float32)

    def add(rows_ref, usable):
        half = rows_ref.shape[-1] // 2
        scores = lax.dot_general(
            rows_ref[:, :half], blocks[...], (((1,), (1,)), ((), ())), preferred_element_type=jnp.float32
        )
        scores = jnp.where(usable, scores * HEAD_DIM**-0.5, NEGATIVE)
        before = stats[0:1, :]
        highest = jnp.maximum(before, jnp.max(scores, axis=0, keepdims=True))
        weights = jnp.where(usable, jnp.exp(scores - highest), 0.0)
        scale = jnp.exp(before - highest)
        stats[0:1, :] = highest
        stats[1:2, :] = stats[1:2, :] * scale + jnp.sum(weights, axis=0, keepdims=True)
        product = lax.dot_general(
            weights.astype(jnp.bfloat16),
            rows_ref[:, half:],
            (((0,), (0,)), ((), ())),
            preferred_element_type=jnp.float32,
        )
        own = jnp.concatenate(
            [
                product[head * per_head : (head + 1) * per_head, head * HEAD_DIM : (head + 1) * HEAD_DIM]
                for head in range(KV_HEADS)
            ],
            axis=0,
        )
        column = jnp.transpose(jnp.broadcast_to(scale, (lanes, lanes)))
        total[...] = total[...] * column + own

    def rows_below(count, rows):
        return lax.broadcasted_iota(jnp.int32, (rows, lanes), 0) < count

    @pl.when(step < cache_tiles)
    def _():
        rows = cache_ref.shape[0]
        add(cache_ref, rows_below(live_ref[0] - step * rows, rows))

    for tile in range(span_tiles):

        @pl.when(step == cache_tiles + tile)
        def _(tile=tile):
            rows = span_ref.shape[0]
            add(span_ref, rows_below(live_ref[1 + tile] * rows, rows))

    @pl.when(step == cache_tiles + span_tiles - 1)
    def _():
        rows = new_ref.shape[0]
        row = lax.broadcasted_iota(jnp.int32, (rows, lanes), 0)
        seen = (lax.broadcasted_iota(jnp.int32, (rows, lanes), 1) % per_head) // (per_head // 2)
        add(new_ref, row <= jnp.where(live_ref[1 + span_tiles] > 0, seen, -1))

        high, low = halves(stats[0:1, :])
        scale = jnp.exp(stats[0:1, :] - (high + low))
        sum_high, sum_low = halves(stats[1:2, :] * scale)
        rows4 = jnp.concatenate(
            [high, low, sum_high, sum_low, jnp.zeros((lanes - 4, lanes), jnp.float32)], axis=0
        )
        by_head = jnp.transpose(rows4)
        value_high, value_low = halves(total[...] * jnp.transpose(jnp.broadcast_to(scale, (lanes, lanes))))
        place = lax.broadcasted_iota(jnp.int32, out_ref.shape, 1)
        tiles = jnp.where(place == 0, value_high[:, None, :], 0.0)
        tiles = jnp.where(place == 1, value_low[:, None, :], tiles)
        tiles = jnp.where(place == 2, by_head[:, None, :], tiles)
        out_ref[...] = tiles.astype(jnp.bfloat16)


def attend(live, queries, cache_rows, span_rows, new_rows):
    block = span_rows.shape[0] // 2
    cache_tiles = cache_rows.shape[0] // block
    span_tiles = span_rows.shape[0] // block
    features = cache_rows.shape[1]
    lanes = queries.shape[0]
    return pl.pallas_call(
        functools.partial(attention_kernel, cache_tiles, span_tiles),
        grid=(cache_tiles + span_tiles,),
        in_specs=[
            pl.BlockSpec(memory_space=pltpu.SMEM),
            pl.BlockSpec((lanes, HEAD_DIM), lambda i: (0, 0)),
            pl.BlockSpec((block, features), lambda i: (jnp.minimum(i, cache_tiles - 1), 0)),
            pl.BlockSpec((block, features), lambda i: (jnp.maximum(i - cache_tiles, 0), 0)),
            pl.BlockSpec(new_rows.shape, lambda i: (0, 0)),
        ],
        out_specs=pl.BlockSpec((lanes, TILE_ROWS, HEAD_DIM), lambda i: (0, 0, 0)),
        out_shape=jax.ShapeDtypeStruct((lanes, TILE_ROWS, HEAD_DIM), jnp.bfloat16),
        scratch_shapes=[
            pltpu.VMEM((lanes, KV_HEADS * HEAD_DIM), jnp.bfloat16),
            pltpu.VMEM((lanes, HEAD_DIM), jnp.float32),
            pltpu.VMEM((8, lanes), jnp.float32),
        ],
        compiler_params=pltpu.CompilerParams(vmem_limit_bytes=40 * 2**20),
        cost_estimate=pl.CostEstimate(flops=2**31, bytes_accessed=2**23, transcendentals=2**18),
    )(live, queries, cache_rows, span_rows, new_rows)


def deal_kernel(count, own_pieces, route_ref, arrived_ref, out_ref, partial, sems):
    whole = pltpu.make_async_copy(arrived_ref.at[:, own_pieces], partial, sems.at[count])
    whole.start()
    out_ref[...] = jnp.zeros_like(out_ref)
    pieces = out_ref.shape[1] - 1

    def block_copy(number):
        return pltpu.make_async_copy(
            arrived_ref.at[route_ref[1, number], pl.ds(route_ref[2, number] * pieces, pieces)],
            out_ref.at[route_ref[0, number], pl.ds(0, pieces)],
            sems.at[number],
        )

    for number in range(count):
        block_copy(number).start()
    whole.wait()
    tiles = partial[...].astype(jnp.float32)
    row = lax.broadcasted_iota(jnp.int32, tiles.shape, 1)
    lane = lax.broadcasted_iota(jnp.int32, tiles.shape, 2)
    highest = jnp.sum(jnp.where((row == 2) & (lane < 2), tiles, 0.0), axis=(1, 2), keepdims=True)
    factor = jnp.exp(highest - jnp.max(highest, axis=0, keepdims=True))
    merged = jnp.sum(tiles * factor, axis=0)
    row = lax.broadcasted_iota(jnp.int32, merged.shape, 0)
    lane = lax.broadcasted_iota(jnp.int32, merged.shape, 1)
    weight = jnp.sum(jnp.where((row == 2) & ((lane == 2) | (lane == 3)), merged, 0.0), axis=(0, 1), keepdims=True)
    value = jnp.sum(jnp.where(row < 2, merged, 0.0), axis=0, keepdims=True) / weight
    result = jnp.broadcast_to(value, merged.shape).astype(out_ref.dtype)
    out_ref[:, pieces] = jnp.broadcast_to(result[None], (out_ref.shape[0],) + result.shape)
    for number in range(count):
        block_copy(number).wait()


def deal(route, arrived, pieces):
    devices = arrived.shape[0]
    count = route.shape[1]
    return pl.pallas_call(
        functools.partial(deal_kernel, count, arrived.shape[1] - 1),
        in_specs=[pl.BlockSpec(memory_space=pltpu.SMEM), pl.BlockSpec(memory_space=pl.ANY)],
        out_specs=pl.BlockSpec(memory_space=pltpu.VMEM),
        out_shape=jax.ShapeDtypeStruct((devices, pieces + 1) + arrived.shape[2:], arrived.dtype),
        scratch_shapes=[
            pltpu.VMEM((devices,) + arrived.shape[2:], arrived.dtype),
            pltpu.SemaphoreType.DMA((count + 1,)),
        ],
        compiler_params=pltpu.CompilerParams(vmem_limit_bytes=40 * 2**20),
        cost_estimate=pl.CostEstimate(flops=2**20, bytes_accessed=2**22, transcendentals=2**8),
    )(route, arrived)


def shards(queries, new_tokens, cache_rows, cache_length, span_rows, slot_blocks, decode_owner):
    devices = lax.axis_size("seq")
    own_index = lax.axis_index("seq")
    slot_count, block_rows, features = span_rows.shape
    step_count = queries.shape[0]
    group = queries.shape[1] // (KV_HEADS * HEAD_DIM)
    pieces = block_rows * features // (devices * TILE_ROWS * HEAD_DIM)
    parts = features // (pieces * HEAD_DIM)

    grouped = queries.reshape(step_count, KV_HEADS, group, HEAD_DIM).transpose(1, 0, 2, 3).reshape(-1, HEAD_DIM)
    own_slots = lax.dynamic_slice_in_dim(slot_blocks, own_index * slot_count, slot_count)
    live = jnp.concatenate(
        [
            jnp.clip(cache_length - own_index * cache_rows.shape[0], 0, cache_rows.shape[0]),
            (own_slots >= 0).astype(jnp.int32),
            (own_index == 0).astype(jnp.int32)[None],
        ]
    )
    new_rows = jnp.pad(new_tokens, ((0, 16 - step_count), (0, 0)))
    partial = attend(live, grouped, cache_rows, span_rows.reshape(-1, features), new_rows)

    shares = span_rows.reshape(slot_count, devices // parts, TILE_ROWS, parts, pieces, HEAD_DIM)
    shares = shares.transpose(1, 3, 0, 4, 2, 5).reshape(devices, slot_count * pieces, TILE_ROWS, HEAD_DIM)
    arrived = lax.all_to_all(jnp.concatenate([shares, partial[:, None]], axis=1), "seq", 0, 0, tiled=True)

    numbers = jnp.arange(decode_owner.shape[0], dtype=jnp.int32)
    holder = jnp.argmax(slot_blocks[None, :] == numbers[:, None], axis=1).astype(jnp.int32)
    route = jnp.stack([decode_owner, holder // slot_count, holder % slot_count])
    dealt = lax.all_to_all(deal(route, arrived, pieces), "seq", 0, 0, tiled=True)

    relaid = dealt[:, :pieces].reshape(devices // parts, parts, pieces, TILE_ROWS, HEAD_DIM)
    relaid = relaid.transpose(0, 3, 1, 2, 4).reshape(1, block_rows, features)
    result = dealt[:, pieces, 0].reshape(KV_HEADS, step_count, group * HEAD_DIM)
    attention = result.transpose(1, 0, 2).reshape(step_count, -1)
    return (attention, relaid)


def solution(mesh):
    placed = (
        P("req", None),
        P("req", None),
        P(("req", "seq"), None),
        P("req"),
        P(("req", "seq"), None, None),
        P("req"),
        P("req"),
    )
    return jax.shard_map(
        shards,
        mesh=mesh,
        in_specs=placed,
        out_specs=(P("req", None), P(("req", "seq"), None, None)),
        check_vma=False,
    )
```

```python
import functools

import jax
import jax.numpy as jnp
from jax import lax
from jax.experimental import pallas as pl
from jax.experimental.pallas import tpu as pltpu
from jax.sharding import PartitionSpec as P

HEAD_DIM = 128
KV_HEADS = 8
NEGATIVE = -(2.0**99)

PLANE_X = 4
PLANE_Y = 4
PAIR = 2
CLUSTERS = 4
CLUSTER = PLANE_Y * PAIR * PLANE_X
RUN = PAIR * PLANE_X
CAPACITIES = (4, 5, 6, 8, 32)
VMEM_LIMIT = 56 * 2**20


def device_at(cluster, position):
    return (position // RUN) * RUN * CLUSTERS + cluster * RUN + position % RUN


def cluster_of(device):
    return (device // RUN) % CLUSTERS


def position_of(device):
    return (device // (RUN * CLUSTERS)) * RUN + device % RUN


def halves(value):
    high = value.astype(jnp.bfloat16).astype(jnp.float32)
    low = (value - high).astype(jnp.bfloat16).astype(jnp.float32)
    return high, low


def packed(value, highest, total):
    shape = (value.shape[0], 8, HEAD_DIM)
    row = lax.broadcasted_iota(jnp.int32, shape, 1)
    lane = lax.broadcasted_iota(jnp.int32, shape, 2)
    value_high, value_low = halves(value)
    numbers = jnp.zeros(shape, jnp.float32)
    for place, part in enumerate(halves(highest) + halves(total)):
        numbers = jnp.where(lane == place, part, numbers)
    tiles = jnp.where(row == 2, numbers, 0.0)
    tiles = jnp.where(row == 0, value_high, tiles)
    return jnp.where(row == 1, value_low, tiles)


def merged(tiles):
    row = lax.broadcasted_iota(jnp.int32, tiles.shape, 2)
    lane = lax.broadcasted_iota(jnp.int32, tiles.shape, 3)
    each = jnp.sum(jnp.where((row == 2) & (lane < 2), tiles, 0.0), axis=(2, 3), keepdims=True)
    highest = jnp.max(each, axis=0, keepdims=True)
    summed = jnp.sum(tiles * jnp.exp(each - highest), axis=0)
    row = lax.broadcasted_iota(jnp.int32, summed.shape, 1)
    lane = lax.broadcasted_iota(jnp.int32, summed.shape, 2)
    value = jnp.sum(jnp.where(row < 2, summed, 0.0), axis=1, keepdims=True)
    total = jnp.sum(
        jnp.where((row == 2) & ((lane == 2) | (lane == 3)), summed, 0.0), axis=(1, 2), keepdims=True
    )
    return value, highest[0], total


def attention_kernel(
    cache_tiles, span_tiles, live_ref, queries_ref, cache_ref, span_ref, new_ref, out_ref, blocks, total, stats
):
    step = pl.program_id(0)
    lanes = queries_ref.shape[0]
    per_head = lanes // KV_HEADS

    @pl.when(step == 0)
    def _():
        owner = lax.broadcasted_iota(jnp.int32, (lanes, HEAD_DIM), 0) // per_head
        queries = queries_ref[...].astype(jnp.float32)
        for head in range(KV_HEADS):
            blocks[:, head * HEAD_DIM : (head + 1) * HEAD_DIM] = jnp.where(owner == head, queries, 0.0).astype(
                jnp.bfloat16
            )
        total[...] = jnp.zeros_like(total)
        stats[0:1, :] = jnp.full((1, lanes), NEGATIVE, jnp.float32)
        stats[1:2, :] = jnp.zeros((1, lanes), jnp.float32)

    def add(rows_ref, usable):
        half = rows_ref.shape[-1] // 2
        scores = lax.dot_general(
            rows_ref[:, :half], blocks[...], (((1,), (1,)), ((), ())), preferred_element_type=jnp.float32
        )
        scores = jnp.where(usable, scores * HEAD_DIM**-0.5, NEGATIVE)
        before = stats[0:1, :]
        highest = jnp.maximum(before, jnp.max(scores, axis=0, keepdims=True))
        weights = jnp.where(usable, jnp.exp(scores - highest), 0.0)
        scale = jnp.exp(before - highest)
        stats[0:1, :] = highest
        stats[1:2, :] = stats[1:2, :] * scale + jnp.sum(weights, axis=0, keepdims=True)
        product = lax.dot_general(
            weights.astype(jnp.bfloat16),
            rows_ref[:, half:],
            (((0,), (0,)), ((), ())),
            preferred_element_type=jnp.float32,
        )
        own = jnp.concatenate(
            [
                product[head * per_head : (head + 1) * per_head, head * HEAD_DIM : (head + 1) * HEAD_DIM]
                for head in range(KV_HEADS)
            ],
            axis=0,
        )
        column = jnp.transpose(jnp.broadcast_to(scale, (lanes, lanes)))
        total[...] = total[...] * column + own

    def rows_below(count, rows):
        return lax.broadcasted_iota(jnp.int32, (rows, lanes), 0) < count

    @pl.when(step < cache_tiles)
    def _():
        rows = cache_ref.shape[0]
        add(cache_ref, rows_below(live_ref[0] - step * rows, rows))

    for tile in range(span_tiles):

        @pl.when(step == cache_tiles + tile)
        def _(tile=tile):
            rows, features = span_ref.shape
            share = rows // out_ref.shape[0]
            out_ref[:, tile * share : (tile + 1) * share, :features] = span_ref[...].reshape(-1, share, features)
            add(span_ref, rows_below(live_ref[1 + tile] * rows, rows))

    @pl.when(step == cache_tiles + span_tiles - 1)
    def _():
        rows, features = new_ref.shape
        row = lax.broadcasted_iota(jnp.int32, (rows, lanes), 0)
        seen = (lax.broadcasted_iota(jnp.int32, (rows, lanes), 1) % per_head) // (per_head // 2)
        add(new_ref, row <= jnp.where(live_ref[1 + span_tiles] > 0, seen, -1))

        high, low = halves(stats[0:1, :])
        scale = jnp.exp(stats[0:1, :] - (high + low))
        by_head = jnp.transpose(
            jnp.concatenate(
                [high + low, stats[1:2, :] * scale, scale, jnp.zeros((lanes - 3, lanes), jnp.float32)], axis=0
            )
        )
        value = total[...] * by_head[:, 2:3]
        tiles = packed(value[:, None, :], by_head[:, None, 0:1], by_head[:, None, 1:2])
        count = out_ref.shape[0]
        out_ref[:, :, features:] = tiles.reshape(count, -1, HEAD_DIM).astype(jnp.bfloat16)


def attend(live, queries, cache_rows, span_rows, new_rows):
    block = span_rows.shape[0] // 2
    cache_tiles = cache_rows.shape[0] // block
    span_tiles = span_rows.shape[0] // block
    features = cache_rows.shape[1]
    lanes = queries.shape[0]
    shape = (CLUSTER, span_rows.shape[0] // CLUSTER, features + HEAD_DIM)
    return pl.pallas_call(
        functools.partial(attention_kernel, cache_tiles, span_tiles),
        grid=(cache_tiles + span_tiles,),
        in_specs=[
            pl.BlockSpec(memory_space=pltpu.SMEM),
            pl.BlockSpec((lanes, HEAD_DIM), lambda i: (0, 0)),
            pl.BlockSpec((block, features), lambda i: (jnp.minimum(i, cache_tiles - 1), 0)),
            pl.BlockSpec((block, features), lambda i: (jnp.maximum(i - cache_tiles, 0), 0)),
            pl.BlockSpec(new_rows.shape, lambda i: (0, 0)),
        ],
        out_specs=pl.BlockSpec(shape, lambda i: (0, 0, 0)),
        out_shape=jax.ShapeDtypeStruct(shape, jnp.bfloat16),
        scratch_shapes=[
            pltpu.VMEM((lanes, KV_HEADS * HEAD_DIM), jnp.bfloat16),
            pltpu.VMEM((lanes, HEAD_DIM), jnp.float32),
            pltpu.VMEM((8, lanes), jnp.float32),
        ],
        compiler_params=pltpu.CompilerParams(vmem_limit_bytes=VMEM_LIMIT),
        cost_estimate=pl.CostEstimate(flops=2**31, bytes_accessed=2**23, transcendentals=2**18),
    )(live, queries, cache_rows, span_rows, new_rows)


def outgoing_kernel(route_ref, arrived_ref, *refs):
    out_refs, (partial, sems) = refs[:-2], refs[-2:]
    count = route_ref.shape[1]
    features = arrived_ref.shape[-1] - HEAD_DIM
    share = arrived_ref.shape[1] // 2
    whole = pltpu.make_async_copy(arrived_ref.at[:, :, pl.ds(features, HEAD_DIM)], partial, sems.at[count])
    whole.start()

    def each(act):
        for number in range(count):
            source = arrived_ref.at[
                route_ref[1, number], pl.ds(route_ref[2, number] * share, share), pl.ds(0, features)
            ]
            for distance in range(1, CLUSTERS):

                @pl.when((route_ref[0, number] > 0) & (route_ref[3, number] == distance))
                def _(source=source, number=number, distance=distance):
                    target = out_refs[distance - 1].at[
                        pl.ds(route_ref[4, number] * share, share), pl.ds(0, features)
                    ]
                    act(pltpu.make_async_copy(source, target, sems.at[number]))

    each(lambda copy: copy.start())
    whole.wait()
    tiles = partial[...].astype(jnp.float32).reshape(partial.shape[0], -1, 8, HEAD_DIM)
    result = packed(*merged(tiles)).reshape(-1, HEAD_DIM).astype(jnp.bfloat16)
    for out_ref in out_refs:
        out_ref[: result.shape[0], features:] = result
    each(lambda copy: copy.wait())


def outgoing(capacity, route, arrived):
    share = arrived.shape[1] // 2
    shape = jax.ShapeDtypeStruct((capacity * share, arrived.shape[2]), arrived.dtype)
    return pl.pallas_call(
        outgoing_kernel,
        in_specs=[pl.BlockSpec(memory_space=pltpu.SMEM), pl.BlockSpec(memory_space=pl.ANY)],
        out_specs=[pl.BlockSpec(memory_space=pltpu.VMEM)] * (CLUSTERS - 1),
        out_shape=[shape] * (CLUSTERS - 1),
        scratch_shapes=[
            pltpu.VMEM(arrived.shape[:2] + (HEAD_DIM,), arrived.dtype),
            pltpu.SemaphoreType.DMA((route.shape[1] + 1,)),
        ],
        compiler_params=pltpu.CompilerParams(vmem_limit_bytes=VMEM_LIMIT),
        cost_estimate=pl.CostEstimate(flops=2**20, bytes_accessed=2**21, transcendentals=2**8),
    )(route, arrived)


def dealt_kernel(route_ref, arrived_ref, sent_ref, *refs):
    from_refs, out_ref, partial, sems = refs[: CLUSTERS - 1], refs[-3], refs[-2], refs[-1]
    count = route_ref.shape[1]
    share, width = out_ref.shape[1:]
    features = width - HEAD_DIM
    tile_rows = partial.shape[1]
    partial_refs = (sent_ref,) + from_refs
    partial_copies = [
        pltpu.make_async_copy(
            ref.at[pl.ds(0, tile_rows), pl.ds(features, HEAD_DIM)], partial.at[place], sems.at[count + place]
        )
        for place, ref in enumerate(partial_refs)
    ]
    for copy in partial_copies:
        copy.start()
    out_ref[...] = jnp.zeros_like(out_ref)

    def each(act):
        for number in range(count):
            target = out_ref.at[route_ref[6, number], slice(None), pl.ds(0, features)]
            sources = [
                arrived_ref.at[
                    route_ref[1, number], pl.ds(route_ref[2, number] * share, share), pl.ds(0, features)
                ]
            ] + [ref.at[pl.ds(route_ref[4, number] * share, share), pl.ds(0, features)] for ref in from_refs]
            for distance, source in enumerate(sources):

                @pl.when((route_ref[5, number] > 0) & (route_ref[3, number] == distance))
                def _(source=source, target=target, number=number):
                    act(pltpu.make_async_copy(source, target, sems.at[number]))

    each(lambda copy: copy.start())
    for copy in partial_copies:
        copy.wait()
    tiles = partial[...].astype(jnp.float32).reshape(CLUSTERS, -1, 8, HEAD_DIM)
    value, _, total = merged(tiles)
    result = value / total
    row = lax.broadcasted_iota(jnp.int32, (share, HEAD_DIM), 0)
    rows = jnp.zeros((share, HEAD_DIM), jnp.float32)
    for place in range(result.shape[0]):
        rows = jnp.where(row == place, result[place], rows)
    rows = rows.astype(out_ref.dtype)
    out_ref[:, :, features:] = jnp.broadcast_to(rows[None], (out_ref.shape[0],) + rows.shape)
    each(lambda copy: copy.wait())


def dealt(route, arrived, sent, received):
    share = arrived.shape[1] // 2
    tile_rows = arrived.shape[1]
    return pl.pallas_call(
        dealt_kernel,
        in_specs=[pl.BlockSpec(memory_space=pltpu.SMEM)] + [pl.BlockSpec(memory_space=pl.ANY)] * (2 + len(received)),
        out_specs=pl.BlockSpec(memory_space=pltpu.VMEM),
        out_shape=jax.ShapeDtypeStruct((CLUSTER, share, arrived.shape[2]), arrived.dtype),
        scratch_shapes=[
            pltpu.VMEM((CLUSTERS, tile_rows, HEAD_DIM), arrived.dtype),
            pltpu.SemaphoreType.DMA((route.shape[1] + CLUSTERS,)),
        ],
        compiler_params=pltpu.CompilerParams(vmem_limit_bytes=VMEM_LIMIT),
        cost_estimate=pl.CostEstimate(flops=2**20, bytes_accessed=2**22, transcendentals=2**8),
    )(route, arrived, sent, *received)


def crossed(capacity, route, arrived):
    sent = outgoing(capacity, route, arrived)
    received = [
        lax.ppermute(
            rows,
            "seq",
            [
                (device_at(cluster, position), device_at((cluster + distance) % CLUSTERS, position))
                for cluster in range(CLUSTERS)
                for position in range(CLUSTER)
            ],
        )
        for distance, rows in enumerate(sent, 1)
    ]
    return dealt(route, arrived, sent[0], received)


def shards(queries, new_tokens, cache_rows, cache_length, span_rows, slot_blocks, decode_owner):
    own_index = lax.axis_index("seq")
    slot_count, block_rows, features = span_rows.shape
    step_count = queries.shape[0]
    group = queries.shape[1] // (KV_HEADS * HEAD_DIM)
    count = decode_owner.shape[0]
    clusters = [[device_at(cluster, position) for position in range(CLUSTER)] for cluster in range(CLUSTERS)]

    grouped = queries.reshape(step_count, KV_HEADS, group, HEAD_DIM).transpose(1, 0, 2, 3).reshape(-1, HEAD_DIM)
    own_slots = lax.dynamic_slice_in_dim(slot_blocks, own_index * slot_count, slot_count)
    live = jnp.concatenate(
        [
            jnp.clip(cache_length - own_index * cache_rows.shape[0], 0, cache_rows.shape[0]),
            (own_slots >= 0).astype(jnp.int32),
            (own_index == 0).astype(jnp.int32)[None],
        ]
    )
    new_rows = jnp.pad(new_tokens, ((0, 16 - step_count), (0, 0)))
    shares = attend(live, grouped, cache_rows, span_rows.reshape(-1, features), new_rows)
    arrived = lax.all_to_all(shares, "seq", 0, 0, axis_index_groups=clusters, tiled=True)

    numbers = jnp.arange(count, dtype=jnp.int32)
    slot = jnp.argmax(slot_blocks[None, :] == numbers[:, None], axis=1).astype(jnp.int32)
    holder = slot // slot_count
    source, target = cluster_of(holder), cluster_of(decode_owner)
    distance = (target - source) % CLUSTERS
    journey = source * CLUSTERS + target
    earlier = (journey[None, :] == journey[:, None]) & (numbers[None, :] < numbers[:, None])
    rank = jnp.sum(earlier.astype(jnp.int32), axis=1)
    own_cluster = cluster_of(own_index)
    route = jnp.stack(
        [
            ((source == own_cluster) & (distance > 0)).astype(jnp.int32),
            position_of(holder),
            slot % slot_count,
            distance,
            rank,
            (target == own_cluster).astype(jnp.int32),
            position_of(decode_owner),
            jnp.zeros_like(rank),
        ]
    )
    needed = jnp.max(jnp.where(distance > 0, rank + 1, 0)).reshape(1)
    needed = jnp.maximum(needed, lax.ppermute(needed, "req", [(0, 1), (1, 0)]))
    choice = jnp.sum((needed > jnp.array(CAPACITIES[:-1], jnp.int32)).astype(jnp.int32))
    shares = lax.switch(
        choice, [functools.partial(crossed, capacity) for capacity in CAPACITIES], route, arrived
    )
    arrived = lax.all_to_all(shares, "seq", 0, 0, axis_index_groups=clusters, tiled=True)

    relaid = arrived[:, :, :features].reshape(1, block_rows, features)
    per_device = step_count * KV_HEADS * group // CLUSTER
    result = arrived[:, :per_device, features:].reshape(KV_HEADS, step_count, group * HEAD_DIM)
    attention = result.transpose(1, 0, 2).reshape(step_count, -1)
    return (attention, relaid)


def solution(mesh):
    placed = (
        P("req", None),
        P("req", None),
        P(("req", "seq"), None),
        P("req"),
        P(("req", "seq"), None, None),
        P("req"),
        P("req"),
    )
    return jax.shard_map(
        shards,
        mesh=mesh,
        in_specs=placed,
        out_specs=(P("req", None), P(("req", "seq"), None, None)),
        check_vma=False,
    )
```

```python
import functools

import jax
import jax.numpy as jnp
from jax import lax
from jax.experimental import pallas as pl
from jax.experimental.pallas import tpu as pltpu
from jax.sharding import PartitionSpec as P

HEAD_DIM = 128
KV_HEADS = 8
NEGATIVE = -(2.0**99)

SIDE_X = 4
SIDE_Y = 4
PAIR = 2
CLUSTERS = 4
CLUSTER = SIDE_Y * PAIR * SIDE_X
HEADS_EACH = 4
TILE = 8
CAPACITIES = tuple((near, far) for near in (4, 5, 6) for far in (3, 4, 5)) + ((8, 8), (32, 32))
VMEM_LIMIT = 56 * 2**20


def coordinates(device):
    y, rest = device // (CLUSTERS * PAIR * SIDE_X), device % (CLUSTERS * PAIR * SIDE_X)
    return y, rest // (PAIR * SIDE_X), (rest // SIDE_X) % PAIR, rest % SIDE_X


def device_at(y, cluster, pair, x):
    return ((y * CLUSTERS + cluster) * PAIR + pair) * SIDE_X + x


def position_of(device):
    y, _, pair, x = coordinates(device)
    return (y * PAIR + pair) * SIDE_X + x


def moved(rows, y=0, cluster=0, pair=0, x=0):
    pairs = []
    for device in range(CLUSTERS * CLUSTER):
        at = coordinates(device)
        to = ((at[0] + y) % SIDE_Y, (at[1] + cluster) % CLUSTERS, (at[2] + pair) % PAIR, (at[3] + x) % SIDE_X)
        pairs.append((device, device_at(*to)))
    return lax.ppermute(rows, "seq", pairs)


def halves(value):
    high = value.astype(jnp.bfloat16).astype(jnp.float32)
    low = (value - high).astype(jnp.bfloat16).astype(jnp.float32)
    return high, low


def packed(value, highest, total):
    shape = (value.shape[0], 8, HEAD_DIM)
    row = lax.broadcasted_iota(jnp.int32, shape, 1)
    lane = lax.broadcasted_iota(jnp.int32, shape, 2)
    value_high, value_low = halves(value)
    numbers = jnp.zeros(shape, jnp.float32)
    for place, part in enumerate(halves(highest) + halves(total)):
        numbers = jnp.where(lane == place, part, numbers)
    tiles = jnp.where(row == 2, numbers, 0.0)
    tiles = jnp.where(row == 0, value_high, tiles)
    return jnp.where(row == 1, value_low, tiles)


def merged(tiles):
    row = lax.broadcasted_iota(jnp.int32, tiles.shape, 2)
    lane = lax.broadcasted_iota(jnp.int32, tiles.shape, 3)
    each = jnp.sum(jnp.where((row == 2) & (lane < 2), tiles, 0.0), axis=(2, 3), keepdims=True)
    highest = jnp.max(each, axis=0, keepdims=True)
    summed = jnp.sum(tiles * jnp.exp(each - highest), axis=0)
    row = lax.broadcasted_iota(jnp.int32, summed.shape, 1)
    lane = lax.broadcasted_iota(jnp.int32, summed.shape, 2)
    value = jnp.sum(jnp.where(row < 2, summed, 0.0), axis=1, keepdims=True)
    total = jnp.sum(
        jnp.where((row == 2) & ((lane == 2) | (lane == 3)), summed, 0.0), axis=(1, 2), keepdims=True
    )
    return value, highest[0], total


def attention_kernel(
    own_ref,
    length_ref,
    slots_ref,
    queries_ref,
    new_ref,
    cache_ref,
    span_ref,
    out_ref,
    spans,
    caches,
    blocks,
    grouped,
    fresh,
    total,
    stats,
    tiles_ref,
    read_sems,
    write_sems,
):
    own = own_ref[0]
    slot_count, positions, share, features = spans.shape
    cache_tiles, rows = caches.shape[:2]
    lanes = grouped.shape[0]
    per_head = lanes // KV_HEADS
    steps = new_ref.shape[0]
    group = per_head // steps

    span_reads = [pltpu.make_async_copy(span_ref.at[s], spans.at[s], read_sems.at[s]) for s in range(slot_count)]
    cache_reads = [
        pltpu.make_async_copy(cache_ref.at[t], caches.at[t], read_sems.at[slot_count + t]) for t in range(cache_tiles)
    ]
    writes = [
        pltpu.make_async_copy(
            spans.at[s], out_ref.at[:, pl.ds(s * share, share), pl.ds(0, features)], write_sems.at[s]
        )
        for s in range(slot_count)
    ]
    for copy in span_reads + cache_reads:
        copy.start()

    for head in range(KV_HEADS):
        for step in range(steps):
            for member in range(group):
                row = head * per_head + step * group + member
                column = (head * group + member) * HEAD_DIM
                grouped[row : row + 1, :] = queries_ref[step : step + 1, column : column + HEAD_DIM].astype(
                    jnp.float32
                )
    owner = lax.broadcasted_iota(jnp.int32, (lanes, HEAD_DIM), 0) // per_head
    for head in range(KV_HEADS):
        blocks[:, head * HEAD_DIM : (head + 1) * HEAD_DIM] = jnp.where(owner == head, grouped[...], 0.0).astype(
            jnp.bfloat16
        )
    fresh[...] = jnp.zeros_like(fresh)
    fresh[0:steps, :] = new_ref[...].astype(jnp.float32)
    total[...] = jnp.zeros_like(total)
    stats[0:1, :] = jnp.full((1, lanes), NEGATIVE, jnp.float32)
    stats[1:2, :] = jnp.zeros((1, lanes), jnp.float32)

    def add(values, usable):
        half = features // 2
        scores = lax.dot_general(
            values[:, :half], blocks[...], (((1,), (1,)), ((), ())), preferred_element_type=jnp.float32
        )
        scores = jnp.where(usable, scores * HEAD_DIM**-0.5, NEGATIVE)
        before = stats[0:1, :]
        highest = jnp.maximum(before, jnp.max(scores, axis=0, keepdims=True))
        weights = jnp.where(usable, jnp.exp(scores - highest), 0.0)
        scale = jnp.exp(before - highest)
        stats[0:1, :] = highest
        stats[1:2, :] = stats[1:2, :] * scale + jnp.sum(weights, axis=0, keepdims=True)
        product = lax.dot_general(
            weights.astype(jnp.bfloat16),
            values[:, half:],
            (((0,), (0,)), ((), ())),
            preferred_element_type=jnp.float32,
        )
        kept = jnp.concatenate(
            [
                product[head * per_head : (head + 1) * per_head, head * HEAD_DIM : (head + 1) * HEAD_DIM]
                for head in range(KV_HEADS)
            ],
            axis=0,
        )
        column = jnp.transpose(jnp.broadcast_to(scale, (lanes, lanes)))
        total[...] = total[...] * column + kept

    def rows_below(count):
        return lax.broadcasted_iota(jnp.int32, (rows, lanes), 0) < count

    for s in range(slot_count):
        span_reads[s].wait()
        writes[s].start()
        held = slots_ref[own * slot_count + s] >= 0
        add(spans[s].reshape(rows, features), rows_below(jnp.where(held, rows, 0)))
    for t in range(cache_tiles):
        cache_reads[t].wait()
        add(caches[t], rows_below(length_ref[0] - (own * cache_tiles + t) * rows))
    row = lax.broadcasted_iota(jnp.int32, (fresh.shape[0], lanes), 0)
    seen = (lax.broadcasted_iota(jnp.int32, row.shape, 1) % per_head) // group
    add(fresh[...].astype(jnp.bfloat16), row <= jnp.where(own == 0, seen, -1))

    high, low = halves(stats[0:1, :])
    scale = jnp.exp(stats[0:1, :] - (high + low))
    by_head = jnp.transpose(
        jnp.concatenate(
            [high + low, stats[1:2, :] * scale, scale, jnp.zeros((lanes - 3, lanes), jnp.float32)], axis=0
        )
    )
    value = total[...] * by_head[:, 2:3]
    tiles = packed(value[:, None, :], by_head[:, None, 0:1], by_head[:, None, 1:2])
    tiles_ref[...] = tiles.reshape(tiles_ref.shape).astype(jnp.bfloat16)
    last = pltpu.make_async_copy(
        tiles_ref, out_ref.at[:, :, pl.ds(features, HEAD_DIM)], write_sems.at[slot_count]
    )
    last.start()
    for copy in writes + [last]:
        copy.wait()


def attend(own_index, cache_length, slot_blocks, queries, new_tokens, cache_rows, span_rows):
    slots, block_rows, features = span_rows.shape
    share = block_rows // CLUSTER
    cache_tiles = cache_rows.shape[0] // block_rows
    lanes = queries.size // HEAD_DIM
    smem = pl.BlockSpec(memory_space=pltpu.SMEM)
    vmem = pl.BlockSpec(memory_space=pltpu.VMEM)
    hbm = pl.BlockSpec(memory_space=pl.ANY)
    return pl.pallas_call(
        attention_kernel,
        in_specs=[smem, smem, smem, vmem, vmem, hbm, hbm],
        out_specs=hbm,
        out_shape=jax.ShapeDtypeStruct((CLUSTER, slots * share, features + HEAD_DIM), span_rows.dtype),
        scratch_shapes=[
            pltpu.VMEM((slots, CLUSTER, share, features), jnp.bfloat16),
            pltpu.VMEM((cache_tiles, block_rows, features), jnp.bfloat16),
            pltpu.VMEM((lanes, KV_HEADS * HEAD_DIM), jnp.bfloat16),
            pltpu.VMEM((lanes, HEAD_DIM), jnp.float32),
            pltpu.VMEM((16, features), jnp.float32),
            pltpu.VMEM((lanes, HEAD_DIM), jnp.float32),
            pltpu.VMEM((8, lanes), jnp.float32),
            pltpu.VMEM((CLUSTER, HEADS_EACH * TILE, HEAD_DIM), jnp.bfloat16),
            pltpu.SemaphoreType.DMA((slots + cache_tiles,)),
            pltpu.SemaphoreType.DMA((slots + 1,)),
        ],
        compiler_params=pltpu.CompilerParams(vmem_limit_bytes=VMEM_LIMIT),
        cost_estimate=pl.CostEstimate(flops=2**31, bytes_accessed=2**23, transcendentals=2**18),
    )(
        own_index.reshape(1),
        cache_length,
        slot_blocks,
        queries,
        new_tokens,
        cache_rows.reshape(cache_tiles, block_rows, features),
        span_rows.reshape(slots, CLUSTER, share, features),
    )


def outgoing_kernel(leaving_ref, arrived_ref, *refs):
    out_refs, (partial, sems) = refs[:-2], refs[-2:]
    share = arrived_ref.shape[1] // 2
    features = arrived_ref.shape[2] - HEAD_DIM
    count = leaving_ref[4, 0]
    whole = pltpu.make_async_copy(
        arrived_ref.at[:, :, pl.ds(features, HEAD_DIM)], partial, sems.at[leaving_ref.shape[1]]
    )
    whole.start()

    def each(act):
        @pl.loop(0, count)
        def _(item):
            source = arrived_ref.at[
                leaving_ref[0, item], pl.ds(leaving_ref[1, item] * share, share), pl.ds(0, features)
            ]
            for distance, out_ref in enumerate(out_refs, 1):

                @pl.when(leaving_ref[2, item] == distance)
                def _(out_ref=out_ref):
                    target = out_ref.at[pl.ds(leaving_ref[3, item] * share, share), pl.ds(0, features)]
                    act(pltpu.make_async_copy(source, target, sems.at[item]))

    each(lambda copy: copy.start())
    whole.wait()
    tiles = partial[...].astype(jnp.float32).reshape(partial.shape[0], -1, TILE, HEAD_DIM)
    result = packed(*merged(tiles)).reshape(-1, HEAD_DIM).astype(jnp.bfloat16)
    for out_ref in out_refs:
        out_ref[: result.shape[0], features:] = result
    each(lambda copy: copy.wait())


def outgoing(capacities, leaving, arrived):
    share = arrived.shape[1] // 2
    return pl.pallas_call(
        outgoing_kernel,
        in_specs=[pl.BlockSpec(memory_space=pltpu.SMEM), pl.BlockSpec(memory_space=pl.ANY)],
        out_specs=[pl.BlockSpec(memory_space=pltpu.VMEM)] * len(capacities),
        out_shape=[
            jax.ShapeDtypeStruct((capacity * share, arrived.shape[2]), arrived.dtype) for capacity in capacities
        ],
        scratch_shapes=[
            pltpu.VMEM(arrived.shape[:2] + (HEAD_DIM,), arrived.dtype),
            pltpu.SemaphoreType.DMA((leaving.shape[1] + 1,)),
        ],
        compiler_params=pltpu.CompilerParams(vmem_limit_bytes=VMEM_LIMIT),
        cost_estimate=pl.CostEstimate(flops=2**20, bytes_accessed=2**21, transcendentals=2**8),
    )(leaving, arrived)


def dealt_kernel(coming_ref, arrived_ref, sent_ref, *refs):
    from_refs, out_ref, sems = refs[:-2], refs[-2], refs[-1]
    share = out_ref.shape[1]
    features = out_ref.shape[2] - HEAD_DIM
    count = coming_ref[5, 0]
    out_ref[...] = jnp.zeros_like(out_ref)

    def near(item):
        return pltpu.make_async_copy(
            arrived_ref.at[coming_ref[0, item], pl.ds(coming_ref[1, item] * share, share), pl.ds(0, features)],
            out_ref.at[coming_ref[4, item], slice(None), pl.ds(0, features)],
            sems.at[item],
        )

    @pl.loop(0, count)
    def _(item):
        @pl.when(coming_ref[2, item] == 0)
        def _():
            near(item).start()

    @pl.loop(0, count)
    def _(item):
        first = pl.multiple_of(coming_ref[3, item] * share, share)
        for distance, ref in enumerate(from_refs, 1):

            @pl.when(coming_ref[2, item] == distance)
            def _(ref=ref):
                out_ref[coming_ref[4, item], :, :features] = ref[pl.ds(first, share), :features]

    rows = HEADS_EACH * TILE
    tiles = jnp.stack([ref[:rows, features:] for ref in (sent_ref,) + from_refs]).astype(jnp.float32)
    value, _, weight = merged(tiles.reshape(CLUSTERS, HEADS_EACH, TILE, HEAD_DIM))
    result = value / weight
    row = lax.broadcasted_iota(jnp.int32, (share, HEAD_DIM), 0)
    lines = jnp.zeros((share, HEAD_DIM), jnp.float32)
    for place in range(HEADS_EACH):
        lines = jnp.where(row == place, result[place], lines)
    lines = lines.astype(out_ref.dtype)
    out_ref[:, :, features:] = jnp.broadcast_to(lines[None], (out_ref.shape[0],) + lines.shape)

    @pl.loop(0, count)
    def _(item):
        @pl.when(coming_ref[2, item] == 0)
        def _():
            near(item).wait()


def dealt(coming, arrived, sent, received):
    share = arrived.shape[1] // 2
    vmem = pl.BlockSpec(memory_space=pltpu.VMEM)
    return pl.pallas_call(
        dealt_kernel,
        in_specs=[pl.BlockSpec(memory_space=pltpu.SMEM), pl.BlockSpec(memory_space=pl.ANY)]
        + [vmem] * (1 + len(received)),
        out_specs=vmem,
        out_shape=jax.ShapeDtypeStruct((CLUSTER, share, arrived.shape[2]), arrived.dtype),
        scratch_shapes=[pltpu.SemaphoreType.DMA((coming.shape[1],))],
        compiler_params=pltpu.CompilerParams(vmem_limit_bytes=VMEM_LIMIT),
        cost_estimate=pl.CostEstimate(flops=2**20, bytes_accessed=2**22, transcendentals=2**8),
    )(coming, arrived, sent, *received)


def crossed(capacities, leaving, coming, arrived):
    near, far = capacities
    sent = outgoing((near, far, near), leaving, arrived)
    received = [moved(rows, cluster=distance) for distance, rows in enumerate(sent, 1)]
    return dealt(coming, arrived, sent[0], received)


def parted_kernel(arrived_ref, attention_ref, relaid_ref, sems):
    features = relaid_ref.shape[2]
    runs = sems.shape[0]
    each = relaid_ref.shape[0] // runs
    copies = [
        pltpu.make_async_copy(
            arrived_ref.at[pl.ds(run * each, each), slice(None), pl.ds(0, features)],
            relaid_ref.at[pl.ds(run * each, each)],
            sems.at[run],
        )
        for run in range(runs)
    ]
    for copy in copies:
        copy.start()
    steps = attention_ref.shape[0]
    group = attention_ref.shape[1] // (KV_HEADS * HEAD_DIM)
    for head in range(KV_HEADS):
        for member in range(group):
            lines = []
            for step in range(steps):
                place = (head * steps + step) * group + member
                tile = arrived_ref[place // HEADS_EACH, :, features:].astype(jnp.float32)
                lines.append(tile[place % HEADS_EACH : place % HEADS_EACH + 1])
            column = (head * group + member) * HEAD_DIM
            attention_ref[:, column : column + HEAD_DIM] = jnp.concatenate(lines).astype(attention_ref.dtype)
    for copy in copies:
        copy.wait()


def parted(arrived, steps):
    positions, share, width = arrived.shape
    features = width - HEAD_DIM
    heads = positions * HEADS_EACH // steps
    return pl.pallas_call(
        parted_kernel,
        in_specs=[pl.BlockSpec(memory_space=pltpu.VMEM)],
        out_specs=[pl.BlockSpec(memory_space=pltpu.VMEM), pl.BlockSpec(memory_space=pl.ANY)],
        out_shape=[
            jax.ShapeDtypeStruct((steps, heads * HEAD_DIM), arrived.dtype),
            jax.ShapeDtypeStruct((positions, share, features), arrived.dtype),
        ],
        scratch_shapes=[pltpu.SemaphoreType.DMA((4,))],
        compiler_params=pltpu.CompilerParams(vmem_limit_bytes=VMEM_LIMIT),
        cost_estimate=pl.CostEstimate(flops=0, bytes_accessed=2**22, transcendentals=0),
    )(arrived)


def compact(valid, columns):
    numbers = jnp.arange(valid.shape[0], dtype=jnp.int32)
    order = jnp.sum((valid[None, :] & (numbers[None, :] < numbers[:, None])).astype(jnp.int32), axis=1)
    chosen = valid[None, :] & (order[None, :] == numbers[:, None])
    rows = [jnp.sum(jnp.where(chosen, column[None, :], 0), axis=1) for column in columns]
    return jnp.stack(rows + [jnp.broadcast_to(jnp.sum(valid.astype(jnp.int32)), numbers.shape)])


def shards(queries, new_tokens, cache_rows, cache_length, span_rows, slot_blocks, decode_owner):
    own_index = lax.axis_index("seq")
    own_cluster = coordinates(own_index)[1]
    slot_count, block_rows, features = span_rows.shape
    count = decode_owner.shape[0]
    clusters = [
        [device_at(y, cluster, pair, x) for y in range(SIDE_Y) for pair in range(PAIR) for x in range(SIDE_X)]
        for cluster in range(CLUSTERS)
    ]

    shares = attend(own_index, cache_length, slot_blocks, queries, new_tokens, cache_rows, span_rows)
    arrived = lax.all_to_all(shares, "seq", 0, 0, axis_index_groups=clusters, tiled=True)

    numbers = jnp.arange(count, dtype=jnp.int32)
    slot = jnp.argmax(slot_blocks[None, :] == numbers[:, None], axis=1).astype(jnp.int32)
    holder = slot // slot_count
    source, target = coordinates(holder)[1], coordinates(decode_owner)[1]
    distance = (target - source) % CLUSTERS
    journey = source * CLUSTERS + target
    earlier = (journey[None, :] == journey[:, None]) & (numbers[None, :] < numbers[:, None])
    rank = jnp.sum(earlier.astype(jnp.int32), axis=1)
    place, kept = position_of(holder), position_of(decode_owner)
    leaving = compact((source == own_cluster) & (distance > 0), [place, slot % slot_count, distance, rank])
    coming = compact(target == own_cluster, [place, slot % slot_count, distance, rank, kept])
    far = distance == CLUSTERS // 2
    needed = jnp.stack(
        [
            jnp.max(jnp.where((distance > 0) & ~far, rank + 1, 0)),
            jnp.max(jnp.where(far, rank + 1, 0)),
        ]
    )
    needed = jnp.maximum(needed, lax.ppermute(needed, "req", [(0, 1), (1, 0)]))
    fits = jnp.all(needed[None, :] <= jnp.array(CAPACITIES, jnp.int32), axis=1)
    shares = lax.switch(
        jnp.argmax(fits).astype(jnp.int32),
        [functools.partial(crossed, capacities) for capacities in CAPACITIES],
        leaving,
        coming,
        arrived,
    )
    arrived = lax.all_to_all(shares, "seq", 0, 0, axis_index_groups=clusters, tiled=True)
    attention, relaid = parted(arrived, queries.shape[0])
    return (attention, relaid.reshape(1, block_rows, features))


def solution(mesh):
    placed = (
        P("req", None),
        P("req", None),
        P(("req", "seq"), None),
        P("req"),
        P(("req", "seq"), None, None),
        P("req"),
        P("req"),
    )
    return jax.shard_map(
        shards,
        mesh=mesh,
        in_specs=placed,
        out_specs=(P("req", None), P(("req", "seq"), None, None)),
        check_vma=False,
    )
```
